32 devices in a mesh: row: 4 (over x, core), col: 8 (over z, y).
Axes of the slice: x: 2, y: 2, z: 4, core: 2. Of those that a mesh axis runs over, the one named last changes fastest.
Arguments:
- nodes: bfloat16 [2048, 512], P(('row', 'col')), may hold values from -6 to 6
- edges: bfloat16 [4, 8, 4096, 512], P('row', 'col'), may hold values from -6 to 6
- senders: int32 [4, 8, 4096], P('row', 'col'), may hold values from 0 to 255
- receivers: int32 [4, 8, 4096], P('row', 'col'), may hold values from 0 to 511
- levels: int32 [4, 8, 4096], P('row', 'col'), may hold values from 0 to 6
- counts: int32 [4, 8], P('row', 'col'), may hold values from 1 to 4096, as said below
- edge_w1: bfloat16 [3, 512, 512], replicated, may hold values from -0.15625 to 0.15625
- level_bias: bfloat16 [7, 512], replicated, may hold values from -6 to 6
- edge_w2: bfloat16 [512, 512], replicated, may hold values from -0.25 to 0.25
- edge_gain: float32 [512], replicated, may hold values from 0.1 to 1.9
- node_w1: bfloat16 [2, 512, 512], replicated, may hold values from -0.1875 to 0.1875
- node_w2: bfloat16 [512, 512], replicated, may hold values from -0.25 to 0.25
- node_gain: float32 [512], replicated, may hold values from 0.1 to 1.9
- grid: bfloat16 [32768, 512], P(('row', 'col')), may hold values from -6 to 6
- send_rows: int32 [32, 32, 4], P(('row', 'col')), may hold values from 0 to 63, as said below
- dec_index: int32 [32768, 3], P(('row', 'col')), may hold values from 0 to 127, as said below
- dec_w1: bfloat16 [2, 512, 512], replicated, may hold values from -0.1875 to 0.1875
- dec_w2: bfloat16 [512, 512], replicated, may hold values from -0.25 to 0.25
- dec_gain: float32 [512], replicated, may hold values from 0.1 to 1.9
Outputs:
- nodes_out: bfloat16 [2048, 512], P(('row', 'col'))
- edges_out: bfloat16 [4, 8, 4096, 512], P('row', 'col')
- grid_out: bfloat16 [32768, 512], P(('row', 'col'))
The draws below stay inside these ranges and needn't reach their ends.
Inputs may be any that keep to these rules, and one draw needn't show every extreme that they name: `senders`: at slots at or beyond the tile's count the index is arbitrary and unused. `receivers`: at slots at or beyond the tile's count the index is arbitrary and unused. `counts`: some tile is full in every draw. `send_rows`: the 4 rows that one device sends to one band device are distinct. `dec_index`: buffer rows are laid out by source device, then slot; every row of a band's buffer is named by some decoder edge of that band.
All inputs are finite; a program needn't handle non-finite values.
Results may differ from the reference program's by a relative error of at most 0.015.
Values may be sent and summed in bfloat16 or wider, within the bound.
A program may use at most 128 MiB of HBM per device.

```python
import jax
import jax.numpy as jnp
from jax import lax

D = 512
LEVELS = 7
KD = 3
NB = 64
RQ = 4
GC = 1024
NODES = 2048
EC = 4096
GRID = 32768
N_ROW = 4
N_COL = 8


def draw_counts(key, part):
    key_spread, key_pick = jax.random.split(jax.random.fold_in(key, 11))
    spread = jax.random.randint(key_spread, (N_ROW, N_COL), 300, 1001)
    filled = spread * spread // 1000 * EC // 1000
    filled = jnp.maximum(filled, 1).reshape(-1)
    chosen = jax.random.randint(key_pick, (), 0, N_ROW * N_COL)
    filled = jnp.where(jnp.arange(N_ROW * N_COL) == chosen, EC, filled)
    return filled.reshape(N_ROW, N_COL).astype(jnp.int32)


def draw_send_rows(key, part):
    device_count = N_ROW * N_COL
    scores = jax.random.randint(jax.random.fold_in(key, 12), (device_count, device_count, NB), 0, 2 ** 20)
    scores = scores * NB + jnp.arange(NB, dtype=jnp.int32)
    values_top, chosen = lax.top_k(scores, RQ)
    return chosen.astype(jnp.int32)


def draw_dec_index(key, part):
    device_count = N_ROW * N_COL
    keys = jax.random.split(jax.random.fold_in(key, 13), device_count)
    orders = jax.vmap(lambda single_key: jax.random.permutation(single_key, GC * KD))(keys)
    return (orders % (device_count * RQ)).reshape(device_count * GC, KD).astype(jnp.int32)


def set_ends(entries, rng, least, top_value):
    longest = entries.shape.index(max(entries.shape))
    spots = []
    for shift in (0, 1):
        where = [jax.random.randint(jax.random.fold_in(rng, axis), (), 0, length) for axis, length in enumerate(entries.shape)]
        where[longest] = (where[longest] + shift) % entries.shape[longest]
        spots.append(tuple(where))
    return entries.at[spots[0]].set(least).at[spots[1]].set(top_value)


def block_levels(key, extent, cuts, low, largest):
    factor_of, own = 1.0, jax.random.fold_in(key, 6)
    for position, shards_of in cuts:
        steps = jnp.exp(jax.random.uniform(jax.random.fold_in(own, position), (shards_of,), jnp.float32, low / len(cuts), largest / len(cuts)))
        factor_of = factor_of * jnp.repeat(steps, extent[position] // shards_of).reshape([-1 if axis == position else 1 for axis in range(len(extent))])
    return factor_of


def bell_draw(rng, shape, scale, most, cuts=(), kind=jnp.bfloat16):
    result = jax.random.normal(rng, shape, jnp.float32) * scale
    if len(cuts) > 0:
        result = block_levels(rng, shape, cuts, -0.22, 0.18) * result
    return jnp.clip(result, min=-most, max=most).astype(kind)


def setup_inputs(seed: int = 0) -> dict:
    key_list = jax.random.split(jax.random.key(seed), 20)
    return {
        "nodes": bell_draw(key_list[0], (NODES, D), 1.0, 6.0, ((0, 32),)),
        "edges": bell_draw(key_list[1], (N_ROW, N_COL, EC, D), 1.0, 6.0, ((0, 4), (1, 8))),
        "senders": set_ends(jax.random.randint(key_list[2], (N_ROW, N_COL, EC), 0, NODES // N_COL), jax.random.fold_in(key_list[2], 1), 0, (NODES // N_COL) - 1).astype(jnp.int32),
        "receivers": set_ends(jax.random.randint(key_list[3], (N_ROW, N_COL, EC), 0, NODES // N_ROW), jax.random.fold_in(key_list[3], 1), 0, (NODES // N_ROW) - 1).astype(jnp.int32),
        "levels": set_ends(jax.random.randint(key_list[4], (N_ROW, N_COL, EC), 0, LEVELS), jax.random.fold_in(key_list[4], 1), 0, LEVELS - 1).astype(jnp.int32),
        "counts": draw_counts(jax.random.fold_in(key_list[19], 71), 0),
        "edge_w1": bell_draw(key_list[6], (3, D, D), (3 * D) ** -0.5, 0.15625),
        "level_bias": bell_draw(key_list[7], (LEVELS, D), 1.0, 6.0),
        "edge_w2": bell_draw(key_list[8], (D, D), D ** -0.5, 0.25),
        "edge_gain": jnp.clip(1.0 + 0.18 * jax.random.normal(key_list[9], (D,), jnp.float32), 0.1, 1.9),
        "node_w1": bell_draw(key_list[10], (2, D, D), (2 * D) ** -0.5, 0.1875),
        "node_w2": bell_draw(key_list[11], (D, D), D ** -0.5, 0.25),
        "node_gain": jnp.clip(1.0 + 0.18 * jax.random.normal(key_list[12], (D,), jnp.float32), 0.1, 1.9),
        "grid": bell_draw(key_list[13], (GRID, D), 1.0, 6.0, ((0, 32),)),
        "send_rows": draw_send_rows(jax.random.fold_in(key_list[19], 71), 0),
        "dec_index": draw_dec_index(jax.random.fold_in(key_list[19], 71), 0),
        "dec_w1": bell_draw(key_list[16], (2, D, D), (2 * D) ** -0.5, 0.1875),
        "dec_w2": bell_draw(key_list[17], (D, D), D ** -0.5, 0.25),
        "dec_gain": jnp.clip(1.0 + 0.18 * jax.random.normal(key_list[18], (D,), jnp.float32), 0.1, 1.9),
    }


EPSILON = 1e-05

def layer_norm(values, gain):
    center = values - lax.optimization_barrier(jnp.mean(values, axis=-1, keepdims=True))
    spread = lax.optimization_barrier(jnp.mean(center * center, axis=-1, keepdims=True))
    return center * lax.rsqrt(spread + EPSILON) * gain

def mlp_tail(pre, second_weight, gain):
    hidden = jax.nn.silu(pre).astype(jnp.bfloat16)
    output = jnp.dot(hidden, second_weight, preferred_element_type=jnp.float32)
    return layer_norm(output, gain)

def reference(nodes, edges, senders, receivers, levels, counts, edge_w1, level_bias, edge_w2, edge_gain, node_w1, node_w2, node_gain, grid, send_rows, dec_index, dec_w1, dec_w2, dec_gain):
    tiles = N_ROW * N_COL
    block = NODES // tiles
    recv_span = NODES // N_ROW
    row_ids = jnp.arange(N_ROW, dtype=jnp.int32)[:, None, None]
    col_ids = jnp.arange(N_COL, dtype=jnp.int32)[None, :, None]
    sender_global = senders // block * (N_COL * block) + col_ids * block + senders % block
    receiver_global = row_ids * recv_span + receivers
    valid = jnp.arange(EC, dtype=jnp.int32)[None, None, :] < counts[:, :, None]
    sender_proj = jnp.dot(nodes, edge_w1[1], preferred_element_type=jnp.float32)
    receiver_proj = jnp.dot(nodes, edge_w1[2], preferred_element_type=jnp.float32)
    level_range = jnp.arange(LEVELS, dtype=jnp.int32)

    def tile_step(total, item):
        edge_rows, send_ids, recv_ids, level_ids, used = item
        onehot = (level_ids[:, None] == level_range[None, :]).astype(jnp.bfloat16)
        pre = jnp.dot(edge_rows, edge_w1[0], preferred_element_type=jnp.float32)
        pre = pre + sender_proj[send_ids] + receiver_proj[recv_ids]
        pre = pre + jnp.dot(onehot, level_bias, preferred_element_type=jnp.float32)
        message = mlp_tail(pre, edge_w2, edge_gain).astype(jnp.bfloat16)
        kept = jnp.where(used[:, None], message.astype(jnp.float32), jnp.zeros((), jnp.float32))
        updated = (edge_rows.astype(jnp.float32) + kept).astype(jnp.bfloat16)
        return (total.at[recv_ids].add(kept), updated)
    items = (edges.reshape(tiles, EC, D), sender_global.reshape(tiles, EC), receiver_global.reshape(tiles, EC), levels.reshape(tiles, EC), valid.reshape(tiles, EC))
    aggregated, edge_new = lax.scan(tile_step, jnp.zeros((NODES, D), jnp.float32), items)
    edges_out = edge_new.reshape(N_ROW, N_COL, EC, D)
    node_pre = jnp.dot(nodes, node_w1[0], preferred_element_type=jnp.float32)
    node_pre = node_pre + jnp.dot(aggregated.astype(jnp.bfloat16), node_w1[1], preferred_element_type=jnp.float32)
    nodes_out = (nodes.astype(jnp.float32) + mlp_tail(node_pre, node_w2, node_gain)).astype(jnp.bfloat16)
    source_ids = jnp.arange(tiles, dtype=jnp.int32)[None, :, None] * block + jnp.transpose(send_rows, (1, 0, 2))
    buffer_global = source_ids.reshape(tiles, tiles * RQ)
    band = jnp.arange(GRID, dtype=jnp.int32) // GC
    cell_senders = buffer_global[band[:, None], dec_index]
    node_dec = jnp.dot(nodes_out, dec_w1[1], preferred_element_type=jnp.float32)
    grid_part = jnp.dot(grid, dec_w1[0], preferred_element_type=jnp.float32)
    dec_pre = grid_part[:, None, :] + node_dec[cell_senders]
    messages = mlp_tail(dec_pre.reshape(GRID * KD, D), dec_w2, dec_gain).reshape(GRID, KD, D)
    grid_out = (grid.astype(jnp.float32) + lax.optimization_barrier(jnp.sum(messages, axis=1))).astype(jnp.bfloat16)
    return (nodes_out, edges_out, grid_out)
```

```python
import functools
import math

import jax
import jax.numpy as jnp
from jax import lax
from jax.experimental import pallas as pl
from jax.experimental.pallas import tpu as pltpu
from jax.sharding import PartitionSpec as P

EPSILON = 1e-05
LANES = 128
MESH = pl.DeviceIdType.MESH
BF16 = jnp.bfloat16
F32 = jnp.float32
VMEM = pl.BlockSpec(memory_space=pltpu.VMEM)


def dot(left, right):
    return jnp.dot(left, right, preferred_element_type=F32)


def halved(weight):
    return (weight.astype(F32) * 0.5).astype(BF16)


def centred(weight):
    wide = weight.astype(F32)
    return (wide - jnp.mean(wide, axis=1, keepdims=True)).astype(BF16)


def silu_half(half):
    return (half + half * jnp.tanh(half)).astype(BF16)


def scaled(center, gain):
    spread = jnp.mean(center * center, axis=-1, keepdims=True)
    return center * lax.rsqrt(spread + EPSILON) * gain


def columns_of(rows):
    count = rows[0].shape[1]
    place = lax.broadcasted_iota(jnp.int32, (8, count), 0)
    joined = jnp.broadcast_to(rows[-1], (8, count))
    for index in range(len(rows) - 1):
        joined = jnp.where(place == index, jnp.broadcast_to(rows[index], (8, count)), joined)
    return joined.T


def hot(column, count):
    shape = (column.shape[0], count)
    return (lax.broadcasted_iota(jnp.int32, shape, 1) == column).astype(F32).astype(BF16)


def gather_kernel(n_row, n_col, nodes_ref, out_ref, send_sem, recv_sem):
    row, col = lax.axis_index("row"), lax.axis_index("col")
    block = nodes_ref.shape[0]
    barrier = pltpu.get_barrier_semaphore()
    for k in range(1, n_row):
        pl.semaphore_signal(barrier, inc=1, device_id=(lax.rem(row + k, n_row), col), device_id_type=MESH)
    for k in range(1, n_col):
        pl.semaphore_signal(barrier, inc=1, device_id=(row, lax.rem(col + k, n_col)), device_id_type=MESH)
    pl.semaphore_wait(barrier, n_row + n_col - 2)

    def slot(index):
        return out_ref.at[pl.ds(pl.multiple_of(index * block, block), block)]

    copies = []
    for k in range(1, n_col):
        copies.append((slot(n_row + col), k, (row, lax.rem(col + k, n_col)), slot(n_row + lax.rem(col + n_col - k, n_col))))
    for k in range(1, n_row):
        copies.append((slot(row), n_col + k, (lax.rem(row + k, n_row), col), slot(lax.rem(row + n_row - k, n_row))))
    started = []
    for target, sem, device, arrival in copies:
        copy = pltpu.make_async_remote_copy(
            nodes_ref, target, send_sem.at[sem], recv_sem.at[sem], device_id=device, device_id_type=MESH
        )
        copy.start()
        started.append(
            pltpu.make_async_remote_copy(
                nodes_ref, arrival, send_sem.at[sem], recv_sem.at[sem], device_id=device, device_id_type=MESH
            )
        )
    own = nodes_ref[...]
    slot(row)[...] = own
    slot(n_row + col)[...] = own
    for copy in started:
        copy.wait()


def edge_kernel(
    sender_count,
    chunk,
    counts_ref,
    edges_ref,
    senders_ref,
    receivers_ref,
    levels_ref,
    gathered_ref,
    w1_ref,
    bias_ref,
    w2_ref,
    gain_ref,
    edges_out_ref,
    partial_ref,
    table_ref,
    first_ref,
    second_ref,
    message_ref,
    total_ref,
):
    step = pl.program_id(0)
    rows = edges_ref.shape[0]
    receiver_count = partial_ref.shape[0]
    known = sender_count + receiver_count

    @pl.when(step == 0)
    def _():
        first_ref[...] = halved(w1_ref[0])
        second_ref[...] = centred(w2_ref[...])
        table_ref[:sender_count] = dot(gathered_ref[:sender_count], halved(w1_ref[1])).astype(BF16)
        table_ref[sender_count:known] = dot(gathered_ref[sender_count:], halved(w1_ref[2])).astype(BF16)
        table_ref[known:] = jnp.zeros((table_ref.shape[0] - known, table_ref.shape[1]), BF16)
        table_ref[known : known + bias_ref.shape[0]] = halved(bias_ref[...])
        total_ref[...] = jnp.zeros_like(total_ref)

    count = counts_ref[0, 0]
    gain = gain_ref[...]
    for part in range(rows // chunk):
        span = pl.ds(part * chunk, chunk)
        ids = columns_of([senders_ref[:, span], receivers_ref[:, span], levels_ref[:, span]])
        chosen = jnp.concatenate(
            [hot(ids[:, 0:1], sender_count), hot(ids[:, 1:2], receiver_count), hot(ids[:, 2:3], LANES)], axis=1
        )
        values = edges_ref[span]
        half = dot(values, first_ref[...]) + dot(chosen, table_ref[...])
        message = scaled(dot(silu_half(half), second_ref[...]), gain).astype(BF16)
        message_ref[span] = message
        place = step * rows + part * chunk + lax.broadcasted_iota(jnp.int32, (chunk, 1), 0)
        kept = jnp.where(place < count, message.astype(F32), 0.0)
        edges_out_ref[span] = (values.astype(F32) + kept).astype(BF16)
    slots = step * rows + lax.broadcasted_iota(jnp.int32, (1, rows), 1)
    targets = jnp.where(slots < count, receivers_ref[...], -1)
    spread = (lax.broadcasted_iota(jnp.int32, (receiver_count, rows), 0) == targets).astype(F32).astype(BF16)
    total_ref[...] += dot(spread, message_ref[...])

    @pl.when(step == pl.num_programs(0) - 1)
    def _():
        partial_ref[...] = total_ref[...].astype(BF16)


def node_kernel(
    n_row,
    n_col,
    partial_ref,
    nodes_ref,
    w1_ref,
    w2_ref,
    gain_ref,
    rows_ref,
    nodes_out_ref,
    band_ref,
    landing_ref,
    picked_ref,
    sum_send,
    sum_recv,
    band_send,
    band_recv,
):
    row, col = lax.axis_index("row"), lax.axis_index("col")
    me = row * n_col + col
    n_dev = n_row * n_col
    block, width = nodes_ref.shape
    pieces = width // LANES
    per_peer = rows_ref.shape[1]
    tile = pieces * per_peer
    barrier = pltpu.get_barrier_semaphore()

    def device(index):
        return (index // n_col, lax.rem(index, n_col))

    def greet(k, carry):
        pl.semaphore_signal(barrier, inc=1, device_id=device(lax.rem(me + k, n_dev)), device_id_type=MESH)
        return carry

    lax.fori_loop(1, n_dev, greet, 0)
    pl.semaphore_wait(barrier, n_dev - 1)

    def sum_copy(k):
        other = lax.rem(col + k, n_col)
        return pltpu.make_async_remote_copy(
            partial_ref.at[pl.ds(pl.multiple_of(other * block, block), block)],
            landing_ref.at[k],
            sum_send.at[k],
            sum_recv.at[k],
            device_id=(row, other),
            device_id_type=MESH,
        )

    for k in range(1, n_col):
        sum_copy(k).start()
    base = dot(nodes_ref[...], halved(w1_ref[0]))
    lower = halved(w1_ref[1])
    second = centred(w2_ref[...])
    count = n_dev * tile
    owner = lax.broadcasted_iota(jnp.int32, (count, n_dev), 0) // tile
    spread = (owner == lax.broadcasted_iota(jnp.int32, (count, n_dev), 1)).astype(F32).astype(BF16)
    wanted = dot(spread, rows_ref[...].astype(F32).astype(BF16))
    which = lax.broadcasted_iota(jnp.int32, (count, per_peer), 0) % per_peer
    wanted = jnp.where(which == lax.broadcasted_iota(jnp.int32, (count, per_peer), 1), wanted, 0.0)
    wanted = jnp.sum(wanted, axis=1, keepdims=True)
    local = lax.broadcasted_iota(jnp.int32, (count, block), 1).astype(F32)
    select = (local == wanted).astype(F32).astype(BF16)
    piece_of = (lax.broadcasted_iota(jnp.int32, (count, LANES), 0) // per_peer) % pieces

    total = partial_ref[pl.ds(pl.multiple_of(col * block, block), block)].astype(F32)
    for k in range(1, n_col):
        sum_copy(k).wait()
        total = total + landing_ref[k].astype(F32)
    half = base + dot(total.astype(BF16), lower)
    fresh = scaled(dot(silu_half(half), second), gain_ref[...])
    fresh = (nodes_ref[...].astype(F32) + fresh).astype(BF16)
    nodes_out_ref[...] = fresh
    selected = jnp.zeros((count, LANES), F32)
    for c in range(pieces):
        selected = jnp.where(piece_of == c, dot(select, fresh[:, c * LANES : (c + 1) * LANES]), selected)
    picked_ref[...] = selected.astype(BF16)

    def part(ref, index):
        return ref.at[pl.ds(pl.multiple_of(index * tile, tile), tile)]

    def send(k, carry):
        other = lax.rem(me + k, n_dev)
        pltpu.make_async_remote_copy(
            part(picked_ref, other),
            part(band_ref, me),
            band_send.at[k],
            band_recv.at[k],
            device_id=device(other),
            device_id_type=MESH,
        ).start()
        return carry

    lax.fori_loop(1, n_dev, send, 0)
    part(band_ref, me)[...] = part(picked_ref, me)[...]

    def finish(k, carry):
        other = lax.rem(me + k, n_dev)
        source = lax.rem(me + n_dev - k, n_dev)
        pltpu.make_async_remote_copy(
            part(picked_ref, other),
            part(band_ref, source),
            band_send.at[k],
            band_recv.at[k],
            device_id=device(other),
            device_id_type=MESH,
        ).wait()
        return carry

    lax.fori_loop(1, n_dev, finish, 0)


def grid_kernel(
    per_peer, grid_ref, index_ref, band_ref, w1_ref, w2_ref, gain_ref, out_ref, first_ref, second_ref, table_ref
):
    count = table_ref.shape[0]
    pieces = grid_ref.shape[1] // LANES
    tile = pieces * per_peer

    @pl.when(pl.program_id(0) == 0)
    def _():
        first_ref[...] = halved(w1_ref[0])
        second_ref[...] = centred(w2_ref[...])
        shape = (count, count * pieces)
        sender = lax.broadcasted_iota(jnp.int32, shape, 0)
        start = sender // per_peer * tile + sender % per_peer
        place = lax.broadcasted_iota(jnp.int32, shape, 1)
        band = band_ref[...]
        table = jnp.zeros(table_ref.shape, F32)
        for c in range(pieces):
            order = (place == start + c * per_peer).astype(F32).astype(BF16)
            piece = dot(order, band).astype(BF16)
            table = table + dot(piece, halved(w1_ref[1, c * LANES : (c + 1) * LANES]))
        table_ref[...] = table.astype(BF16)

    values = grid_ref[...]
    gain = gain_ref[...]
    fan = index_ref.shape[0]
    ids = columns_of([index_ref[e : e + 1] for e in range(fan)])
    base = dot(values, first_ref[...])
    total = values.astype(F32)
    for e in range(fan):
        half = base + dot(hot(ids[:, e : e + 1], count), table_ref[...])
        total = total + scaled(dot(silu_half(half), second_ref[...]), gain)
    out_ref[...] = total.astype(BF16)


def whole(shape):
    return pl.BlockSpec(shape, lambda i: (0,) * len(shape))


def on_device(
    n_row,
    n_col,
    nodes,
    edges,
    senders,
    receivers,
    levels,
    counts,
    edge_w1,
    level_bias,
    edge_w2,
    edge_gain,
    node_w1,
    node_w2,
    node_gain,
    grid,
    send_rows,
    dec_index,
    dec_w1,
    dec_w2,
    dec_gain,
):
    block, width = nodes.shape
    capacity = edges.shape[2]
    n_dev = n_row * n_col
    sender_count, receiver_count = block * n_row, block * n_col
    known = sender_count + receiver_count

    gathered = pl.pallas_call(
        functools.partial(gather_kernel, n_row, n_col),
        out_shape=jax.ShapeDtypeStruct((known, width), BF16),
        in_specs=[VMEM],
        out_specs=VMEM,
        scratch_shapes=[pltpu.SemaphoreType.DMA((n_row + n_col,)), pltpu.SemaphoreType.DMA((n_row + n_col,))],
        compiler_params=pltpu.CompilerParams(
            collective_id=0, has_side_effects=True, vmem_limit_bytes=16 * 2**20
        ),
        name="gather_nodes",
    )(nodes)

    rows = math.gcd(capacity, 1024)
    chunk = math.gcd(rows, 256)
    table_rows = known + LANES

    def id_spec():
        return pl.BlockSpec((1, rows), lambda i: (0, i))

    edge_new, partial = pl.pallas_call(
        functools.partial(edge_kernel, sender_count, chunk),
        grid=(capacity // rows,),
        out_shape=(
            jax.ShapeDtypeStruct((capacity, width), BF16),
            jax.ShapeDtypeStruct((receiver_count, width), BF16),
        ),
        in_specs=[
            pl.BlockSpec(memory_space=pltpu.SMEM),
            pl.BlockSpec((rows, width), lambda i: (i, 0)),
            id_spec(),
            id_spec(),
            id_spec(),
            whole((known, width)),
            whole(edge_w1.shape),
            whole(level_bias.shape),
            whole(edge_w2.shape),
            whole((1, width)),
        ],
        out_specs=(pl.BlockSpec((rows, width), lambda i: (i, 0)), whole((receiver_count, width))),
        scratch_shapes=[
            pltpu.VMEM((table_rows, width), BF16),
            pltpu.VMEM((width, width), BF16),
            pltpu.VMEM((width, width), BF16),
            pltpu.VMEM((rows, width), BF16),
            pltpu.VMEM((receiver_count, width), F32),
        ],
        compiler_params=pltpu.CompilerParams(vmem_limit_bytes=44 * 2**20),
        name="edge_update",
    )(
        counts,
        edges.reshape(capacity, width),
        senders.reshape(1, capacity),
        receivers.reshape(1, capacity),
        levels.reshape(1, capacity),
        gathered,
        edge_w1,
        level_bias,
        edge_w2,
        edge_gain.reshape(1, width),
    )

    peers, per_peer = send_rows.shape[1:]
    tile = per_peer * (width // LANES)
    nodes_out, band = pl.pallas_call(
        functools.partial(node_kernel, n_row, n_col),
        out_shape=(
            jax.ShapeDtypeStruct((block, width), BF16),
            jax.ShapeDtypeStruct((peers * tile, LANES), BF16),
        ),
        in_specs=[VMEM] * 6,
        out_specs=(VMEM, VMEM),
        scratch_shapes=[
            pltpu.VMEM((n_col, block, width), BF16),
            pltpu.VMEM((peers * tile, LANES), BF16),
            pltpu.SemaphoreType.DMA((n_col,)),
            pltpu.SemaphoreType.DMA((n_col,)),
            pltpu.SemaphoreType.DMA((n_dev,)),
            pltpu.SemaphoreType.DMA((n_dev,)),
        ],
        compiler_params=pltpu.CompilerParams(
            collective_id=1, has_side_effects=True, vmem_limit_bytes=24 * 2**20
        ),
        name="node_update",
    )(partial, nodes, node_w1, node_w2, node_gain.reshape(1, width), send_rows.reshape(peers, per_peer))

    cells, fan = dec_index.shape
    cell_rows = math.gcd(cells, 256)
    grid_out = pl.pallas_call(
        functools.partial(grid_kernel, per_peer),
        grid=(cells // cell_rows,),
        out_shape=jax.ShapeDtypeStruct((cells, width), BF16),
        in_specs=[
            pl.BlockSpec((cell_rows, width), lambda i: (i, 0)),
            pl.BlockSpec((fan, cell_rows), lambda i: (0, i)),
            whole((peers * tile, LANES)),
            whole(dec_w1.shape),
            whole(dec_w2.shape),
            whole((1, width)),
        ],
        out_specs=pl.BlockSpec((cell_rows, width), lambda i: (i, 0)),
        scratch_shapes=[
            pltpu.VMEM((width, width), BF16),
            pltpu.VMEM((width, width), BF16),
            pltpu.VMEM((peers * per_peer, width), BF16),
        ],
        compiler_params=pltpu.CompilerParams(vmem_limit_bytes=40 * 2**20),
        name="grid_update",
    )(grid, dec_index.T, band, dec_w1, dec_w2, dec_gain.reshape(1, width))
    return (nodes_out, edge_new.reshape(edges.shape), grid_out)


def solution(mesh):
    return jax.shard_map(
        functools.partial(on_device, mesh.shape["row"], mesh.shape["col"]),
        mesh=mesh,
        in_specs=(
            P(("row", "col"), None),
            P("row", "col", None, None),
            P("row", "col", None),
            P("row", "col", None),
            P("row", "col", None),
            P("row", "col"),
            P(),
            P(),
            P(),
            P(),
            P(),
            P(),
            P(),
            P(("row", "col"), None),
            P(("row", "col"), None, None),
            P(("row", "col"), None),
            P(),
            P(),
            P(),
        ),
        out_specs=(P(("row", "col"), None), P("row", "col", None, None), P(("row", "col"), None)),
        check_vma=False,
    )
```

```python
import functools
import math

import jax
import jax.numpy as jnp
from jax import lax
from jax.experimental import pallas as pl
from jax.experimental.pallas import tpu as pltpu
from jax.sharding import PartitionSpec as P

EPSILON = 1e-05
LANES = 128
MESH = pl.DeviceIdType.MESH
BF16 = jnp.bfloat16
F32 = jnp.float32
VMEM = pl.BlockSpec(memory_space=pltpu.VMEM)
ANY = pl.BlockSpec(memory_space=pl.ANY)
VMEM_LIMIT = 60 * 2**20


def dot(left, right):
    return jnp.dot(left, right, preferred_element_type=F32)


def halved(weight):
    return (weight.astype(F32) * 0.5).astype(BF16)


def centred(weight):
    wide = weight.astype(F32)
    return (wide - jnp.mean(wide, axis=1, keepdims=True)).astype(BF16)


def silu_half(half):
    return (half + half * jnp.tanh(half)).astype(BF16)


def scaled(center, gain):
    spread = jnp.mean(center * center, axis=-1, keepdims=True)
    return center * lax.rsqrt(spread + EPSILON) * gain


def columns_of(rows):
    count = rows[0].shape[1]
    place = lax.broadcasted_iota(jnp.int32, (8, count), 0)
    joined = jnp.broadcast_to(rows[-1], (8, count))
    for index in range(len(rows) - 1):
        joined = jnp.where(place == index, jnp.broadcast_to(rows[index], (8, count)), joined)
    return joined.T


def hot(column, count):
    shape = (column.shape[0], count)
    return (lax.broadcasted_iota(jnp.int32, shape, 1) == column).astype(F32).astype(BF16)


def split_of(n_col):
    outer = math.gcd(n_col, 4)
    return outer, n_col // outer


def gather_kernel(n_row, n_col, nodes_ref, out_ref, send_sem, recv_sem):
    row, col = lax.axis_index("row"), lax.axis_index("col")
    outer, inner = split_of(n_col)
    high, low = col // inner, lax.rem(col, inner)
    block = nodes_ref.shape[0]

    def out_dev(k):
        return (row, lax.rem(high + k, outer) * inner + low)

    def in_dev(m):
        return (row, high * inner + lax.rem(low + m, inner))

    def row_dev(k):
        return (lax.rem(row + k, n_row), col)

    barrier = pltpu.get_barrier_semaphore()
    friends = [out_dev(k) for k in range(1, outer)] + [in_dev(m) for m in range(1, inner)]
    friends += [row_dev(k) for k in range(1, n_row)]
    for friend in friends:
        pl.semaphore_signal(barrier, inc=1, device_id=friend, device_id_type=MESH)
    pl.semaphore_wait(barrier, len(friends))

    def slot(index):
        return out_ref.at[pl.ds(pl.multiple_of(index * block, block), block)]

    def col_slot(k, m):
        return slot(n_row + lax.rem(high + outer - k, outer) * inner + lax.rem(low + inner - m, inner))

    def copy(source, target, sem, device):
        return pltpu.make_async_remote_copy(
            source, target, send_sem.at[sem], recv_sem.at[sem], device_id=device, device_id_type=MESH
        )

    waits = []
    for k in range(1, outer):
        copy(nodes_ref, slot(n_row + col), k * inner, out_dev(k)).start()
    for m in range(1, inner):
        copy(nodes_ref, slot(n_row + col), m, in_dev(m)).start()
        waits.append(copy(nodes_ref, col_slot(0, m), m, in_dev(m)))
    for k in range(1, n_row):
        copy(nodes_ref, slot(row), n_col + k, row_dev(k)).start()
        waits.append(copy(nodes_ref, slot(lax.rem(row + n_row - k, n_row)), n_col + k, row_dev(k)))
    own = nodes_ref[...]
    slot(row)[...] = own
    slot(n_row + col)[...] = own
    for k in range(1, outer):
        arrived = copy(nodes_ref, col_slot(k, 0), k * inner, out_dev(k))
        arrived.wait()
        for m in range(1, inner):
            copy(col_slot(k, 0), col_slot(k, 0), k * inner + m, in_dev(m)).start()
            waits.append(copy(col_slot(k, 0), col_slot(k, m), k * inner + m, in_dev(m)))
    for wait in waits:
        wait.wait()


def edge_kernel(
    sender_count,
    chunk,
    counts_ref,
    edges_ref,
    senders_ref,
    receivers_ref,
    levels_ref,
    gathered_ref,
    w1_ref,
    bias_ref,
    w2_ref,
    gain_ref,
    edges_out_ref,
    partial_ref,
    table_ref,
    first_ref,
    second_ref,
    message_ref,
    total_ref,
):
    step = pl.program_id(0)
    rows = edges_ref.shape[0]
    receiver_count = partial_ref.shape[0]
    known = sender_count + receiver_count

    @pl.when(step == 0)
    def _():
        first_ref[...] = halved(w1_ref[0])
        second_ref[...] = centred(w2_ref[...])
        table_ref[:sender_count] = dot(gathered_ref[:sender_count], halved(w1_ref[1])).astype(BF16)
        table_ref[sender_count:known] = dot(gathered_ref[sender_count:], halved(w1_ref[2])).astype(BF16)
        table_ref[known:] = jnp.zeros((table_ref.shape[0] - known, table_ref.shape[1]), BF16)
        table_ref[known : known + bias_ref.shape[0]] = halved(bias_ref[...])
        total_ref[...] = jnp.zeros_like(total_ref)

    count = counts_ref[0, 0]
    gain = gain_ref[...]
    for part in range(rows // chunk):
        span = pl.ds(part * chunk, chunk)
        ids = columns_of([senders_ref[:, span], receivers_ref[:, span], levels_ref[:, span]])
        chosen = jnp.concatenate(
            [hot(ids[:, 0:1], sender_count), hot(ids[:, 1:2], receiver_count), hot(ids[:, 2:3], LANES)], axis=1
        )
        values = edges_ref[span]
        half = dot(values, first_ref[...]) + dot(chosen, table_ref[...])
        message = scaled(dot(silu_half(half), second_ref[...]), gain).astype(BF16)
        message_ref[span] = message
        place = step * rows + part * chunk + lax.broadcasted_iota(jnp.int32, (chunk, 1), 0)
        kept = jnp.where(place < count, message.astype(F32), 0.0)
        edges_out_ref[span] = (values.astype(F32) + kept).astype(BF16)
    slots = step * rows + lax.broadcasted_iota(jnp.int32, (1, rows), 1)
    targets = jnp.where(slots < count, receivers_ref[...], -1)
    spread = (lax.broadcasted_iota(jnp.int32, (receiver_count, rows), 0) == targets).astype(F32).astype(BF16)
    total_ref[...] += dot(spread, message_ref[...])

    @pl.when(step == pl.num_programs(0) - 1)
    def _():
        partial_ref[...] = total_ref[...].astype(BF16)


def node_kernel(
    n_row,
    n_col,
    partial_ref,
    nodes_ref,
    w1_hbm,
    w2_hbm,
    gain_ref,
    rows_ref,
    nodes_out_ref,
    band_ref,
    w1_ref,
    w2_ref,
    near_ref,
    stage_ref,
    far_ref,
    picked_ref,
    load_sem,
    near_send,
    near_recv,
    far_send,
    far_recv,
    band_send,
    band_recv,
):
    row, col = lax.axis_index("row"), lax.axis_index("col")
    outer, inner = split_of(n_col)
    high, low = col // inner, lax.rem(col, inner)
    me = row * n_col + col
    n_dev = n_row * n_col
    block, width = nodes_ref.shape
    pieces = width // LANES
    per_peer = rows_ref.shape[1]
    tile = pieces * per_peer
    barrier = pltpu.get_barrier_semaphore()

    def device(index):
        return (index // n_col, lax.rem(index, n_col))

    def greet(k, carry):
        pl.semaphore_signal(barrier, inc=1, device_id=device(lax.rem(me + k, n_dev)), device_id_type=MESH)
        return carry

    lax.fori_loop(1, n_dev, greet, 0)
    load_first = pltpu.make_async_copy(w1_hbm, w1_ref, load_sem.at[0])
    load_second = pltpu.make_async_copy(w2_hbm, w2_ref, load_sem.at[1])
    load_first.start()
    load_second.start()
    pl.semaphore_wait(barrier, n_dev - 1)

    def sums(k, m):
        index = lax.rem(high + k, outer) * inner + lax.rem(low + m, inner)
        return partial_ref.at[pl.ds(pl.multiple_of(index * block, block), block)]

    def near_copy(k, m):
        return pltpu.make_async_remote_copy(
            sums(k, m),
            near_ref.at[k * inner + m],
            near_send.at[k * inner + m],
            near_recv.at[k * inner + m],
            device_id=(row, high * inner + lax.rem(low + m, inner)),
            device_id_type=MESH,
        )

    def far_copy(k):
        return pltpu.make_async_remote_copy(
            stage_ref.at[k],
            far_ref.at[k],
            far_send.at[k],
            far_recv.at[k],
            device_id=(row, lax.rem(high + k, outer) * inner + low),
            device_id_type=MESH,
        )

    order = list(range(1, outer)) + [0]
    for k in order:
        for m in range(1, inner):
            near_copy(k, m).start()
    count = n_dev * tile
    owner = lax.broadcasted_iota(jnp.int32, (count, n_dev), 0) // tile
    spread = (owner == lax.broadcasted_iota(jnp.int32, (count, n_dev), 1)).astype(F32).astype(BF16)
    wanted = dot(spread, rows_ref[...].astype(F32).astype(BF16))
    which = lax.broadcasted_iota(jnp.int32, (count, per_peer), 0) % per_peer
    wanted = jnp.where(which == lax.broadcasted_iota(jnp.int32, (count, per_peer), 1), wanted, 0.0)
    wanted = jnp.sum(wanted, axis=1, keepdims=True)
    local = lax.broadcasted_iota(jnp.int32, (count, block), 1).astype(F32)
    select = (local == wanted).astype(F32).astype(BF16)
    piece_of = (lax.broadcasted_iota(jnp.int32, (count, LANES), 0) // per_peer) % pieces

    total = None
    for k in order:
        total = sums(k, 0)[...].astype(F32)
        for m in range(1, inner):
            near_copy(k, m).wait()
            total = total + near_ref[k * inner + m].astype(F32)
        if k > 0:
            stage_ref[k] = total.astype(BF16)
            far_copy(k).start()
    load_first.wait()
    load_second.wait()
    base = dot(nodes_ref[...], halved(w1_ref[0]))
    lower = halved(w1_ref[1])
    second = centred(w2_ref[...])
    for k in range(1, outer):
        far_copy(k).wait()
        total = total + far_ref[k].astype(F32)
    half = base + dot(total.astype(BF16), lower)
    fresh = scaled(dot(silu_half(half), second), gain_ref[...])
    fresh = (nodes_ref[...].astype(F32) + fresh).astype(BF16)
    nodes_out_ref[...] = fresh
    selected = jnp.zeros((count, LANES), F32)
    for c in range(pieces):
        selected = jnp.where(piece_of == c, dot(select, fresh[:, c * LANES : (c + 1) * LANES]), selected)
    picked_ref[...] = selected.astype(BF16)

    def part(ref, index):
        return ref.at[pl.ds(pl.multiple_of(index * tile, tile), tile)]

    def send(k, carry):
        other = lax.rem(me + k, n_dev)
        pltpu.make_async_remote_copy(
            part(picked_ref, other),
            part(band_ref, me),
            band_send.at[k],
            band_recv.at[k],
            device_id=device(other),
            device_id_type=MESH,
        ).start()
        return carry

    lax.fori_loop(1, n_dev, send, 0)
    part(band_ref, me)[...] = part(picked_ref, me)[...]

    def finish(k, carry):
        other = lax.rem(me + k, n_dev)
        source = lax.rem(me + n_dev - k, n_dev)
        pltpu.make_async_remote_copy(
            part(picked_ref, other),
            part(band_ref, source),
            band_send.at[k],
            band_recv.at[k],
            device_id=device(other),
            device_id_type=MESH,
        ).wait()
        return carry

    lax.fori_loop(1, n_dev, finish, 0)


def grid_kernel(
    per_peer,
    grid_ref,
    index_ref,
    band_ref,
    w1_ref,
    w2_ref,
    gain_ref,
    nodes_ref,
    out_ref,
    nodes_out_ref,
    first_ref,
    second_ref,
    table_ref,
):
    count = table_ref.shape[0]
    pieces = grid_ref.shape[1] // LANES
    tile = pieces * per_peer

    @pl.when(pl.program_id(0) == 0)
    def _():
        nodes_out_ref[...] = nodes_ref[...]
        first_ref[...] = halved(w1_ref[0])
        second_ref[...] = centred(w2_ref[...])
        shape = (count, count * pieces)
        sender = lax.broadcasted_iota(jnp.int32, shape, 0)
        start = sender // per_peer * tile + sender % per_peer
        place = lax.broadcasted_iota(jnp.int32, shape, 1)
        band = band_ref[...]
        table = jnp.zeros(table_ref.shape, F32)
        for c in range(pieces):
            order = (place == start + c * per_peer).astype(F32).astype(BF16)
            piece = dot(order, band).astype(BF16)
            table = table + dot(piece, halved(w1_ref[1, c * LANES : (c + 1) * LANES]))
        table_ref[...] = table.astype(BF16)

    values = grid_ref[...]
    gain = gain_ref[...]
    fan = index_ref.shape[0]
    ids = columns_of([index_ref[e : e + 1] for e in range(fan)])
    base = dot(values, first_ref[...])
    total = values.astype(F32)
    for e in range(fan):
        half = base + dot(hot(ids[:, e : e + 1], count), table_ref[...])
        total = total + scaled(dot(silu_half(half), second_ref[...]), gain)
    out_ref[...] = total.astype(BF16)


def whole(shape):
    return pl.BlockSpec(shape, lambda i: (0,) * len(shape))


def on_device(
    n_row,
    n_col,
    nodes,
    edges,
    senders,
    receivers,
    levels,
    counts,
    edge_w1,
    level_bias,
    edge_w2,
    edge_gain,
    node_w1,
    node_w2,
    node_gain,
    grid,
    send_rows,
    dec_index,
    dec_w1,
    dec_w2,
    dec_gain,
):
    block, width = nodes.shape
    capacity = edges.shape[2]
    n_dev = n_row * n_col
    sender_count, receiver_count = block * n_row, block * n_col
    known = sender_count + receiver_count

    gathered = pl.pallas_call(
        functools.partial(gather_kernel, n_row, n_col),
        out_shape=jax.ShapeDtypeStruct((known, width), BF16),
        in_specs=[VMEM],
        out_specs=VMEM,
        scratch_shapes=[pltpu.SemaphoreType.DMA((n_row + n_col,))] * 2,
        compiler_params=pltpu.CompilerParams(
            collective_id=0, has_side_effects=True, vmem_limit_bytes=VMEM_LIMIT
        ),
        name="gather_nodes",
    )(nodes)

    rows = math.gcd(capacity, 1024)
    chunk = math.gcd(rows, 256)
    table_rows = known + LANES

    def id_spec():
        return pl.BlockSpec((1, rows), lambda i: (0, i))

    edge_new, partial = pl.pallas_call(
        functools.partial(edge_kernel, sender_count, chunk),
        grid=(capacity // rows,),
        out_shape=(
            jax.ShapeDtypeStruct((capacity, width), BF16),
            jax.ShapeDtypeStruct((receiver_count, width), BF16),
        ),
        in_specs=[
            pl.BlockSpec(memory_space=pltpu.SMEM),
            pl.BlockSpec((rows, width), lambda i: (i, 0)),
            id_spec(),
            id_spec(),
            id_spec(),
            whole((known, width)),
            whole(edge_w1.shape),
            whole(level_bias.shape),
            whole(edge_w2.shape),
            whole((1, width)),
        ],
        out_specs=(pl.BlockSpec((rows, width), lambda i: (i, 0)), whole((receiver_count, width))),
        scratch_shapes=[
            pltpu.VMEM((table_rows, width), BF16),
            pltpu.VMEM((width, width), BF16),
            pltpu.VMEM((width, width), BF16),
            pltpu.VMEM((rows, width), BF16),
            pltpu.VMEM((receiver_count, width), F32),
        ],
        compiler_params=pltpu.CompilerParams(vmem_limit_bytes=VMEM_LIMIT),
        name="edge_update",
    )(
        counts,
        edges.reshape(capacity, width),
        senders.reshape(1, capacity),
        receivers.reshape(1, capacity),
        levels.reshape(1, capacity),
        gathered,
        edge_w1,
        level_bias,
        edge_w2,
        edge_gain.reshape(1, width),
    )

    peers, per_peer = send_rows.shape[1:]
    tile = per_peer * (width // LANES)
    outer = split_of(n_col)[0]
    fresh_nodes, band = pl.pallas_call(
        functools.partial(node_kernel, n_row, n_col),
        out_shape=(
            jax.ShapeDtypeStruct((block, width), BF16),
            jax.ShapeDtypeStruct((peers * tile, LANES), BF16),
        ),
        in_specs=[VMEM, VMEM, ANY, ANY, VMEM, VMEM],
        out_specs=(VMEM, VMEM),
        scratch_shapes=[
            pltpu.VMEM(node_w1.shape, BF16),
            pltpu.VMEM(node_w2.shape, BF16),
            pltpu.VMEM((n_col, block, width), BF16),
            pltpu.VMEM((outer, block, width), BF16),
            pltpu.VMEM((outer, block, width), BF16),
            pltpu.VMEM((peers * tile, LANES), BF16),
            pltpu.SemaphoreType.DMA((2,)),
            pltpu.SemaphoreType.DMA((n_col,)),
            pltpu.SemaphoreType.DMA((n_col,)),
            pltpu.SemaphoreType.DMA((outer,)),
            pltpu.SemaphoreType.DMA((outer,)),
            pltpu.SemaphoreType.DMA((n_dev,)),
            pltpu.SemaphoreType.DMA((n_dev,)),
        ],
        compiler_params=pltpu.CompilerParams(
            collective_id=1, has_side_effects=True, vmem_limit_bytes=VMEM_LIMIT
        ),
        name="node_update",
    )(partial, nodes, node_w1, node_w2, node_gain.reshape(1, width), send_rows.reshape(peers, per_peer))

    cells, fan = dec_index.shape
    cell_rows = math.gcd(cells, 256)
    grid_out, nodes_out = pl.pallas_call(
        functools.partial(grid_kernel, per_peer),
        grid=(cells // cell_rows,),
        out_shape=(
            jax.ShapeDtypeStruct((cells, width), BF16),
            jax.ShapeDtypeStruct((block, width), BF16),
        ),
        in_specs=[
            pl.BlockSpec((cell_rows, width), lambda i: (i, 0)),
            pl.BlockSpec((fan, cell_rows), lambda i: (0, i)),
            whole((peers * tile, LANES)),
            whole(dec_w1.shape),
            whole(dec_w2.shape),
            whole((1, width)),
            whole((block, width)),
        ],
        out_specs=(pl.BlockSpec((cell_rows, width), lambda i: (i, 0)), whole((block, width))),
        scratch_shapes=[
            pltpu.VMEM((width, width), BF16),
            pltpu.VMEM((width, width), BF16),
            pltpu.VMEM((peers * per_peer, width), BF16),
        ],
        compiler_params=pltpu.CompilerParams(vmem_limit_bytes=VMEM_LIMIT),
        name="grid_update",
    )(grid, dec_index.T, band, dec_w1, dec_w2, dec_gain.reshape(1, width), fresh_nodes)
    return (nodes_out, edge_new.reshape(edges.shape), grid_out)


def solution(mesh):
    return jax.shard_map(
        functools.partial(on_device, mesh.shape["row"], mesh.shape["col"]),
        mesh=mesh,
        in_specs=(
            P(("row", "col"), None),
            P("row", "col", None, None),
            P("row", "col", None),
            P("row", "col", None),
            P("row", "col", None),
            P("row", "col"),
            P(),
            P(),
            P(),
            P(),
            P(),
            P(),
            P(),
            P(("row", "col"), None),
            P(("row", "col"), None, None),
            P(("row", "col"), None),
            P(),
            P(),
            P(),
        ),
        out_specs=(P(("row", "col"), None), P("row", "col", None, None), P(("row", "col"), None)),
        check_vma=False,
    )
```

```python
import functools
import math

import jax
import jax.numpy as jnp
from jax import lax
from jax.experimental import pallas as pl
from jax.experimental.pallas import tpu as pltpu
from jax.sharding import PartitionSpec as P

EPSILON = 1e-05
LANES = 128
MESH = pl.DeviceIdType.MESH
BF16 = jnp.bfloat16
F32 = jnp.float32
VMEM = pl.BlockSpec(memory_space=pltpu.VMEM)
ANY = pl.BlockSpec(memory_space=pl.ANY)
VMEM_LIMIT = 60 * 2**20


def dot(left, right):
    return jnp.dot(left, right, preferred_element_type=F32)


def halved(weight):
    return (weight.astype(F32) * 0.5).astype(BF16)


def centred(weight):
    wide = weight.astype(F32)
    return (wide - jnp.mean(wide, axis=1, keepdims=True)).astype(BF16)


def silu_half(half):
    return (half + half * jnp.tanh(half)).astype(BF16)


def scaled(center, gain):
    spread = jnp.mean(center * center, axis=-1, keepdims=True)
    return center * lax.rsqrt(spread + EPSILON) * gain


def columns_of(rows):
    count = rows[0].shape[1]
    place = lax.broadcasted_iota(jnp.int32, (8, count), 0)
    joined = jnp.broadcast_to(rows[-1], (8, count))
    for index in range(len(rows) - 1):
        joined = jnp.where(place == index, jnp.broadcast_to(rows[index], (8, count)), joined)
    return joined.T


def hot(column, count):
    shape = (column.shape[0], count)
    return (lax.broadcasted_iota(jnp.int32, shape, 1) == column).astype(F32).astype(BF16)


def split_of(n_col):
    outer = math.gcd(n_col, 4)
    return outer, n_col // outer


def gather_kernel(
    n_row,
    n_col,
    nodes_ref,
    edges_hbm,
    levels_ref,
    w1_hbm,
    bias_ref,
    w2_hbm,
    table_ref,
    second_ref,
    own_hbm,
    out_ref,
    w1_ref,
    w2_ref,
    edges_ref,
    own_ref,
    send_sem,
    recv_sem,
    weight_sem,
    load_sem,
    store_sem,
):
    row, col = lax.axis_index("row"), lax.axis_index("col")
    outer, inner = split_of(n_col)
    high, low = col // inner, lax.rem(col, inner)
    block = nodes_ref.shape[0]

    def out_dev(k):
        return (row, lax.rem(high + k, outer) * inner + low)

    def in_dev(m):
        return (row, high * inner + lax.rem(low + m, inner))

    def row_dev(k):
        return (lax.rem(row + k, n_row), col)

    barrier = pltpu.get_barrier_semaphore()
    friends = [out_dev(k) for k in range(1, outer)] + [in_dev(m) for m in range(1, inner)]
    friends += [row_dev(k) for k in range(1, n_row)]
    for friend in friends:
        pl.semaphore_signal(barrier, inc=1, device_id=friend, device_id_type=MESH)
    load_first = pltpu.make_async_copy(w1_hbm, w1_ref, weight_sem.at[0])
    load_second = pltpu.make_async_copy(w2_hbm, w2_ref, weight_sem.at[1])
    load_first.start()
    stages, rows = edges_ref.shape[:2]

    def load(b):
        return pltpu.make_async_copy(edges_hbm.at[pl.ds(b * rows, rows)], edges_ref.at[b], load_sem.at[b])

    def store(b):
        return pltpu.make_async_copy(own_ref.at[b], own_hbm.at[pl.ds(b * rows, rows)], store_sem.at[b])

    for b in range(stages):
        load(b).start()
    load_second.start()
    pl.semaphore_wait(barrier, len(friends))

    def slot(index):
        return out_ref.at[pl.ds(pl.multiple_of(index * block, block), block)]

    def col_slot(k, m):
        return slot(n_row + lax.rem(high + outer - k, outer) * inner + lax.rem(low + inner - m, inner))

    def copy(source, target, sem, device):
        return pltpu.make_async_remote_copy(
            source, target, send_sem.at[sem], recv_sem.at[sem], device_id=device, device_id_type=MESH
        )

    waits = []
    for k in range(1, outer):
        copy(nodes_ref, slot(n_row + col), k * inner, out_dev(k)).start()
    for m in range(1, inner):
        copy(nodes_ref, slot(n_row + col), m, in_dev(m)).start()
        waits.append(copy(nodes_ref, col_slot(0, m), m, in_dev(m)))
    for k in range(1, n_row):
        copy(nodes_ref, slot(row), n_col + k, row_dev(k)).start()
        waits.append(copy(nodes_ref, slot(lax.rem(row + n_row - k, n_row)), n_col + k, row_dev(k)))
    own = nodes_ref[...]
    slot(row)[...] = own
    slot(n_row + col)[...] = own
    load_first.wait()
    first = halved(w1_ref[0])
    bias = jnp.concatenate(
        [halved(bias_ref[...]), jnp.zeros((LANES - bias_ref.shape[0], bias_ref.shape[1]), BF16)], axis=0
    )

    def own_part(b):
        load(b).wait()
        ids = columns_of([levels_ref[:, pl.ds(b * rows, rows)]])
        own_ref[b] = (dot(edges_ref[b], first) + dot(hot(ids[:, 0:1], LANES), bias)).astype(BF16)
        store(b).start()

    arrivals = outer - 1
    for b in range(stages - arrivals if stages > arrivals else 0):
        own_part(b)
    for k in range(1, outer):
        arrived = copy(nodes_ref, col_slot(k, 0), k * inner, out_dev(k))
        arrived.wait()
        for m in range(1, inner):
            copy(col_slot(k, 0), col_slot(k, 0), k * inner + m, in_dev(m)).start()
            waits.append(copy(col_slot(k, 0), col_slot(k, m), k * inner + m, in_dev(m)))
        b = stages - outer + k
        if b >= 0:
            own_part(b)
    load_second.wait()
    second_ref[...] = centred(w2_ref[...])
    middle, last = halved(w1_ref[1]), halved(w1_ref[2])
    for wait in waits:
        wait.wait()
    known = n_row * block
    table_ref[:known] = dot(out_ref[:known], middle).astype(BF16)
    table_ref[known:] = dot(out_ref[known:], last).astype(BF16)
    for b in range(stages):
        store(b).wait()


def edge_kernel(
    sender_count,
    chunk,
    counts_ref,
    edges_ref,
    own_ref,
    senders_ref,
    receivers_ref,
    table_ref,
    second_ref,
    gain_ref,
    edges_out_ref,
    partial_ref,
    message_ref,
    total_ref,
):
    step = pl.program_id(0)
    rows = edges_ref.shape[0]
    receiver_count = partial_ref.shape[0]

    @pl.when(step == 0)
    def _():
        total_ref[...] = jnp.zeros_like(total_ref)

    count = counts_ref[0, 0]
    gain = gain_ref[...]
    for part in range(rows // chunk):
        span = pl.ds(part * chunk, chunk)
        ids = columns_of([senders_ref[:, span], receivers_ref[:, span]])
        chosen = jnp.concatenate(
            [hot(ids[:, 0:1], sender_count), hot(ids[:, 1:2], receiver_count)], axis=1
        )
        values = edges_ref[span]
        half = own_ref[span].astype(F32) + dot(chosen, table_ref[...])
        message = scaled(dot(silu_half(half), second_ref[...]), gain).astype(BF16)
        message_ref[span] = message
        place = step * rows + part * chunk + lax.broadcasted_iota(jnp.int32, (chunk, 1), 0)
        kept = jnp.where(place < count, message.astype(F32), 0.0)
        edges_out_ref[span] = (values.astype(F32) + kept).astype(BF16)
    slots = step * rows + lax.broadcasted_iota(jnp.int32, (1, rows), 1)
    targets = jnp.where(slots < count, receivers_ref[...], -1)
    spread = (lax.broadcasted_iota(jnp.int32, (receiver_count, rows), 0) == targets).astype(F32).astype(BF16)
    total_ref[...] += dot(spread, message_ref[...])

    @pl.when(step == pl.num_programs(0) - 1)
    def _():
        partial_ref[...] = total_ref[...].astype(BF16)


def node_kernel(
    n_row,
    n_col,
    partial_ref,
    nodes_ref,
    w1_hbm,
    w2_hbm,
    gain_ref,
    rows_ref,
    nodes_out_ref,
    band_ref,
    w1_ref,
    w2_ref,
    near_ref,
    stage_ref,
    far_ref,
    picked_ref,
    load_sem,
    near_send,
    near_recv,
    far_send,
    far_recv,
    band_send,
    band_recv,
):
    row, col = lax.axis_index("row"), lax.axis_index("col")
    outer, inner = split_of(n_col)
    high, low = col // inner, lax.rem(col, inner)
    me = row * n_col + col
    n_dev = n_row * n_col
    block, width = nodes_ref.shape
    pieces = width // LANES
    per_peer = rows_ref.shape[0]
    tile = pieces * per_peer
    barrier = pltpu.get_barrier_semaphore()

    def device(index):
        return (index // n_col, lax.rem(index, n_col))

    def greet(k, carry):
        pl.semaphore_signal(barrier, inc=1, device_id=device(lax.rem(me + k, n_dev)), device_id_type=MESH)
        return carry

    lax.fori_loop(1, n_dev, greet, 0)
    load_first = pltpu.make_async_copy(w1_hbm, w1_ref, load_sem.at[0])
    load_second = pltpu.make_async_copy(w2_hbm, w2_ref, load_sem.at[1])
    load_first.start()
    load_second.start()
    pl.semaphore_wait(barrier, n_dev - 1)

    def sums(k, m):
        index = lax.rem(high + k, outer) * inner + lax.rem(low + m, inner)
        return partial_ref.at[pl.ds(pl.multiple_of(index * block, block), block)]

    def near_copy(k, m):
        return pltpu.make_async_remote_copy(
            sums(k, m),
            near_ref.at[k * inner + m],
            near_send.at[k * inner + m],
            near_recv.at[k * inner + m],
            device_id=(row, high * inner + lax.rem(low + m, inner)),
            device_id_type=MESH,
        )

    def far_copy(k):
        return pltpu.make_async_remote_copy(
            stage_ref.at[k],
            far_ref.at[k],
            far_send.at[k],
            far_recv.at[k],
            device_id=(row, lax.rem(high + k, outer) * inner + low),
            device_id_type=MESH,
        )

    order = list(range(1, outer)) + [0]
    for k in order:
        for m in range(1, inner):
            near_copy(k, m).start()
    count = n_dev * tile
    owner = lax.broadcasted_iota(jnp.int32, (count, n_dev), 0) // tile
    spread = (owner == lax.broadcasted_iota(jnp.int32, (count, n_dev), 1)).astype(F32).astype(BF16)
    wanted = lax.dot_general(
        spread,
        rows_ref[...].astype(F32).astype(BF16),
        (((1,), (1,)), ((), ())),
        preferred_element_type=F32,
    )
    which = lax.broadcasted_iota(jnp.int32, (count, per_peer), 0) % per_peer
    wanted = jnp.where(which == lax.broadcasted_iota(jnp.int32, (count, per_peer), 1), wanted, 0.0)
    wanted = jnp.sum(wanted, axis=1, keepdims=True)
    local = lax.broadcasted_iota(jnp.int32, (count, block), 1).astype(F32)
    select = (local == wanted).astype(F32).astype(BF16)
    piece_of = (lax.broadcasted_iota(jnp.int32, (count, LANES), 0) // per_peer) % pieces

    total = None
    for k in order:
        total = sums(k, 0)[...].astype(F32)
        for m in range(1, inner):
            near_copy(k, m).wait()
            total = total + near_ref[k * inner + m].astype(F32)
        if k > 0:
            stage_ref[k] = total.astype(BF16)
            far_copy(k).start()
    load_first.wait()
    load_second.wait()
    base = dot(nodes_ref[...], halved(w1_ref[0]))
    lower = halved(w1_ref[1])
    second = centred(w2_ref[...])
    for k in range(1, outer):
        far_copy(k).wait()
        total = total + far_ref[k].astype(F32)
    half = base + dot(total.astype(BF16), lower)
    fresh = scaled(dot(silu_half(half), second), gain_ref[...])
    fresh = (nodes_ref[...].astype(F32) + fresh).astype(BF16)
    nodes_out_ref[...] = fresh
    selected = jnp.zeros((count, LANES), F32)
    for c in range(pieces):
        selected = jnp.where(piece_of == c, dot(select, fresh[:, c * LANES : (c + 1) * LANES]), selected)
    picked_ref[...] = selected.astype(BF16)

    def part(ref, index):
        return ref.at[pl.ds(pl.multiple_of(index * tile, tile), tile)]

    def send(k, carry):
        other = lax.rem(me + k, n_dev)
        pltpu.make_async_remote_copy(
            part(picked_ref, other),
            part(band_ref, me),
            band_send.at[k],
            band_recv.at[k],
            device_id=device(other),
            device_id_type=MESH,
        ).start()
        return carry

    lax.fori_loop(1, n_dev, send, 0)
    part(band_ref, me)[...] = part(picked_ref, me)[...]

    def finish(k, carry):
        other = lax.rem(me + k, n_dev)
        source = lax.rem(me + n_dev - k, n_dev)
        pltpu.make_async_remote_copy(
            part(picked_ref, other),
            part(band_ref, source),
            band_send.at[k],
            band_recv.at[k],
            device_id=device(other),
            device_id_type=MESH,
        ).wait()
        return carry

    lax.fori_loop(1, n_dev, finish, 0)


def grid_kernel(
    per_peer,
    grid_ref,
    index_ref,
    band_ref,
    w1_ref,
    w2_ref,
    gain_ref,
    nodes_ref,
    out_ref,
    nodes_out_ref,
    first_ref,
    second_ref,
    table_ref,
):
    count = table_ref.shape[0]
    pieces = grid_ref.shape[1] // LANES
    tile = pieces * per_peer

    @pl.when(pl.program_id(0) == 0)
    def _():
        nodes_out_ref[...] = nodes_ref[...]
        first_ref[...] = halved(w1_ref[0])
        second_ref[...] = centred(w2_ref[...])
        shape = (count, count * pieces)
        sender = lax.broadcasted_iota(jnp.int32, shape, 0)
        start = sender // per_peer * tile + sender % per_peer
        place = lax.broadcasted_iota(jnp.int32, shape, 1)
        band = band_ref[...]
        table = jnp.zeros(table_ref.shape, F32)
        for c in range(pieces):
            order = (place == start + c * per_peer).astype(F32).astype(BF16)
            piece = dot(order, band).astype(BF16)
            table = table + dot(piece, halved(w1_ref[1, c * LANES : (c + 1) * LANES]))
        table_ref[...] = table.astype(BF16)

    values = grid_ref[...]
    gain = gain_ref[...]
    fan = index_ref.shape[0]
    ids = columns_of([index_ref[e : e + 1] for e in range(fan)])
    base = dot(values, first_ref[...])
    total = values.astype(F32)
    for e in range(fan):
        half = base + dot(hot(ids[:, e : e + 1], count), table_ref[...])
        total = total + scaled(dot(silu_half(half), second_ref[...]), gain)
    out_ref[...] = total.astype(BF16)


def whole(shape):
    return pl.BlockSpec(shape, lambda i: (0,) * len(shape))


def on_device(
    n_row,
    n_col,
    nodes,
    edges,
    senders,
    receivers,
    levels,
    counts,
    edge_w1,
    level_bias,
    edge_w2,
    edge_gain,
    node_w1,
    node_w2,
    node_gain,
    grid,
    send_rows,
    dec_index,
    dec_w1,
    dec_w2,
    dec_gain,
):
    block, width = nodes.shape
    capacity = edges.shape[2]
    n_dev = n_row * n_col
    sender_count, receiver_count = block * n_row, block * n_col
    known = sender_count + receiver_count

    rows = math.gcd(capacity, 1024)
    chunk = math.gcd(rows, 256)
    stages = capacity // rows
    flat = edges.reshape(capacity, width)
    outer, inner = split_of(n_col)
    copies = n_row + n_col

    table, second, own = pl.pallas_call(
        functools.partial(gather_kernel, n_row, n_col),
        out_shape=(
            jax.ShapeDtypeStruct((known, width), BF16),
            jax.ShapeDtypeStruct((width, width), BF16),
            jax.ShapeDtypeStruct((capacity, width), BF16),
        ),
        in_specs=[VMEM, ANY, VMEM, ANY, VMEM, ANY],
        out_specs=(VMEM, VMEM, ANY),
        scratch_shapes=[
            pltpu.VMEM((known, width), BF16),
            pltpu.VMEM(edge_w1.shape, BF16),
            pltpu.VMEM(edge_w2.shape, BF16),
            pltpu.VMEM((stages, rows, width), BF16),
            pltpu.VMEM((stages, rows, width), BF16),
            pltpu.SemaphoreType.DMA((copies,)),
            pltpu.SemaphoreType.DMA((copies,)),
            pltpu.SemaphoreType.DMA((2,)),
            pltpu.SemaphoreType.DMA((stages,)),
            pltpu.SemaphoreType.DMA((stages,)),
        ],
        compiler_params=pltpu.CompilerParams(
            collective_id=0, has_side_effects=True, vmem_limit_bytes=VMEM_LIMIT
        ),
        name="gather_nodes",
    )(nodes, flat, levels.reshape(1, capacity), edge_w1, level_bias, edge_w2)

    def id_spec():
        return pl.BlockSpec((1, rows), lambda i: (0, i))

    edge_new, partial = pl.pallas_call(
        functools.partial(edge_kernel, sender_count, chunk),
        grid=(capacity // rows,),
        out_shape=(
            jax.ShapeDtypeStruct((capacity, width), BF16),
            jax.ShapeDtypeStruct((receiver_count, width), BF16),
        ),
        in_specs=[
            pl.BlockSpec(memory_space=pltpu.SMEM),
            pl.BlockSpec((rows, width), lambda i: (i, 0)),
            pl.BlockSpec((rows, width), lambda i: (i, 0)),
            id_spec(),
            id_spec(),
            whole((known, width)),
            whole((width, width)),
            whole((1, width)),
        ],
        out_specs=(pl.BlockSpec((rows, width), lambda i: (i, 0)), whole((receiver_count, width))),
        scratch_shapes=[
            pltpu.VMEM((rows, width), BF16),
            pltpu.VMEM((receiver_count, width), F32),
        ],
        compiler_params=pltpu.CompilerParams(vmem_limit_bytes=VMEM_LIMIT),
        name="edge_update",
    )(
        counts,
        flat,
        own,
        senders.reshape(1, capacity),
        receivers.reshape(1, capacity),
        table,
        second,
        edge_gain.reshape(1, width),
    )

    peers, per_peer = send_rows.shape[1:]
    tile = per_peer * (width // LANES)
    fresh_nodes, band = pl.pallas_call(
        functools.partial(node_kernel, n_row, n_col),
        out_shape=(
            jax.ShapeDtypeStruct((block, width), BF16),
            jax.ShapeDtypeStruct((peers * tile, LANES), BF16),
        ),
        in_specs=[VMEM, VMEM, ANY, ANY, VMEM, VMEM],
        out_specs=(VMEM, VMEM),
        scratch_shapes=[
            pltpu.VMEM(node_w1.shape, BF16),
            pltpu.VMEM(node_w2.shape, BF16),
            pltpu.VMEM((n_col, block, width), BF16),
            pltpu.VMEM((outer, block, width), BF16),
            pltpu.VMEM((outer, block, width), BF16),
            pltpu.VMEM((peers * tile, LANES), BF16),
            pltpu.SemaphoreType.DMA((2,)),
            pltpu.SemaphoreType.DMA((n_col,)),
            pltpu.SemaphoreType.DMA((n_col,)),
            pltpu.SemaphoreType.DMA((outer,)),
            pltpu.SemaphoreType.DMA((outer,)),
            pltpu.SemaphoreType.DMA((n_dev,)),
            pltpu.SemaphoreType.DMA((n_dev,)),
        ],
        compiler_params=pltpu.CompilerParams(
            collective_id=1, has_side_effects=True, vmem_limit_bytes=VMEM_LIMIT
        ),
        name="node_update",
    )(partial, nodes, node_w1, node_w2, node_gain.reshape(1, width), send_rows[0].T)

    cells, fan = dec_index.shape
    cell_rows = math.gcd(cells, 256)
    grid_out, nodes_out = pl.pallas_call(
        functools.partial(grid_kernel, per_peer),
        grid=(cells // cell_rows,),
        out_shape=(
            jax.ShapeDtypeStruct((cells, width), BF16),
            jax.ShapeDtypeStruct((block, width), BF16),
        ),
        in_specs=[
            pl.BlockSpec((cell_rows, width), lambda i: (i, 0)),
            pl.BlockSpec((fan, cell_rows), lambda i: (0, i)),
            whole((peers * tile, LANES)),
            whole(dec_w1.shape),
            whole(dec_w2.shape),
            whole((1, width)),
            whole((block, width)),
        ],
        out_specs=(pl.BlockSpec((cell_rows, width), lambda i: (i, 0)), whole((block, width))),
        scratch_shapes=[
            pltpu.VMEM((width, width), BF16),
            pltpu.VMEM((width, width), BF16),
            pltpu.VMEM((peers * per_peer, width), BF16),
        ],
        compiler_params=pltpu.CompilerParams(vmem_limit_bytes=VMEM_LIMIT),
        name="grid_update",
    )(grid, dec_index.T, band, dec_w1, dec_w2, dec_gain.reshape(1, width), fresh_nodes)
    return (nodes_out, edge_new.reshape(edges.shape), grid_out)


def solution(mesh):
    return jax.shard_map(
        functools.partial(on_device, mesh.shape["row"], mesh.shape["col"]),
        mesh=mesh,
        in_specs=(
            P(("row", "col"), None),
            P("row", "col", None, None),
            P("row", "col", None),
            P("row", "col", None),
            P("row", "col", None),
            P("row", "col"),
            P(),
            P(),
            P(),
            P(),
            P(),
            P(),
            P(),
            P(("row", "col"), None),
            P(("row", "col"), None, None),
            P(("row", "col"), None),
            P(),
            P(),
            P(),
        ),
        out_specs=(P(("row", "col"), None), P("row", "col", None, None), P(("row", "col"), None)),
        check_vma=False,
    )
```

```python
import functools
import math

import jax
import jax.numpy as jnp
from jax import lax
from jax.experimental import pallas as pl
from jax.experimental.pallas import tpu as pltpu
from jax.sharding import PartitionSpec as P

EPSILON = 1e-05
LANES = 128
MESH = pl.DeviceIdType.MESH
BF16 = jnp.bfloat16
F32 = jnp.float32
VMEM = pl.BlockSpec(memory_space=pltpu.VMEM)
ANY = pl.BlockSpec(memory_space=pl.ANY)
VMEM_LIMIT = 60 * 2**20


def dot(left, right):
    return jnp.dot(left, right, preferred_element_type=F32)


def halved(weight):
    return (weight.astype(F32) * 0.5).astype(BF16)


def centred(weight):
    wide = weight.astype(F32)
    return (wide - jnp.mean(wide, axis=1, keepdims=True)).astype(BF16)


def silu_half(half):
    return (half + half * jnp.tanh(half)).astype(BF16)


def scaled(center, gain):
    spread = jnp.mean(center * center, axis=-1, keepdims=True)
    return center * lax.rsqrt(spread + EPSILON) * gain


def columns_of(rows):
    count = rows[0].shape[1]
    place = lax.broadcasted_iota(jnp.int32, (8, count), 0)
    joined = jnp.broadcast_to(rows[-1], (8, count))
    for index in range(len(rows) - 1):
        joined = jnp.where(place == index, jnp.broadcast_to(rows[index], (8, count)), joined)
    return joined.T


def hot(column, count):
    shape = (column.shape[0], count)
    return (lax.broadcasted_iota(jnp.int32, shape, 1) == column).astype(F32).astype(BF16)


def split_of(n_col):
    outer = math.gcd(n_col, 4)
    return outer, n_col // outer


def gather_kernel(
    n_row,
    n_col,
    nodes_ref,
    edges_hbm,
    levels_ref,
    w1_hbm,
    bias_ref,
    w2_hbm,
    table_ref,
    second_ref,
    own_hbm,
    out_ref,
    w1_ref,
    w2_ref,
    edges_ref,
    own_ref,
    send_sem,
    recv_sem,
    weight_sem,
    load_sem,
    store_sem,
):
    row, col = lax.axis_index("row"), lax.axis_index("col")
    outer, inner = split_of(n_col)
    high, low = col // inner, lax.rem(col, inner)
    block = nodes_ref.shape[0]

    def out_dev(k):
        return (row, lax.rem(high + k, outer) * inner + low)

    def in_dev(m):
        return (row, high * inner + lax.rem(low + m, inner))

    def row_dev(k):
        return (lax.rem(row + k, n_row), col)

    barrier = pltpu.get_barrier_semaphore()
    friends = [out_dev(k) for k in range(1, outer)] + [in_dev(m) for m in range(1, inner)]
    friends += [row_dev(k) for k in range(1, n_row)]
    for friend in friends:
        pl.semaphore_signal(barrier, inc=1, device_id=friend, device_id_type=MESH)
    load_first = pltpu.make_async_copy(w1_hbm, w1_ref, weight_sem.at[0])
    load_second = pltpu.make_async_copy(w2_hbm, w2_ref, weight_sem.at[1])
    load_first.start()
    stages, rows = edges_ref.shape[:2]

    def load(b):
        return pltpu.make_async_copy(edges_hbm.at[pl.ds(b * rows, rows)], edges_ref.at[b], load_sem.at[b])

    def store(b):
        return pltpu.make_async_copy(own_ref.at[b], own_hbm.at[pl.ds(b * rows, rows)], store_sem.at[b])

    for b in range(stages):
        load(b).start()
    load_second.start()
    pl.semaphore_wait(barrier, len(friends))

    def slot(index):
        return out_ref.at[pl.ds(pl.multiple_of(index * block, block), block)]

    def col_slot(k, m):
        return slot(n_row + lax.rem(high + outer - k, outer) * inner + lax.rem(low + inner - m, inner))

    def copy(source, target, sem, device):
        return pltpu.make_async_remote_copy(
            source, target, send_sem.at[sem], recv_sem.at[sem], device_id=device, device_id_type=MESH
        )

    waits = []
    for k in range(1, outer):
        copy(nodes_ref, slot(n_row + col), k * inner, out_dev(k)).start()
    for m in range(1, inner):
        copy(nodes_ref, slot(n_row + col), m, in_dev(m)).start()
        waits.append(copy(nodes_ref, col_slot(0, m), m, in_dev(m)))
    for k in range(1, n_row):
        copy(nodes_ref, slot(row), n_col + k, row_dev(k)).start()
        waits.append(copy(nodes_ref, slot(lax.rem(row + n_row - k, n_row)), n_col + k, row_dev(k)))
    own = nodes_ref[...]
    slot(row)[...] = own
    slot(n_row + col)[...] = own
    load_first.wait()
    first = halved(w1_ref[0])
    bias = jnp.concatenate(
        [halved(bias_ref[...]), jnp.zeros((LANES - bias_ref.shape[0], bias_ref.shape[1]), BF16)], axis=0
    )

    def own_part(b):
        load(b).wait()
        ids = columns_of([levels_ref[:, pl.ds(b * rows, rows)]])
        own_ref[b] = (dot(edges_ref[b], first) + dot(hot(ids[:, 0:1], LANES), bias)).astype(BF16)
        store(b).start()

    arrivals = outer - 1
    for b in range(stages - arrivals if stages > arrivals else 0):
        own_part(b)
    for k in range(1, outer):
        arrived = copy(nodes_ref, col_slot(k, 0), k * inner, out_dev(k))
        arrived.wait()
        for m in range(1, inner):
            copy(col_slot(k, 0), col_slot(k, 0), k * inner + m, in_dev(m)).start()
            waits.append(copy(col_slot(k, 0), col_slot(k, m), k * inner + m, in_dev(m)))
        b = stages - outer + k
        if b >= 0:
            own_part(b)
    load_second.wait()
    second_ref[...] = centred(w2_ref[...])
    middle, last = halved(w1_ref[1]), halved(w1_ref[2])
    for wait in waits:
        wait.wait()
    known = n_row * block
    table_ref[:known] = dot(out_ref[:known], middle).astype(BF16)
    table_ref[known:] = dot(out_ref[known:], last).astype(BF16)
    for b in range(stages):
        store(b).wait()


def edge_kernel(
    sender_count,
    chunk,
    counts_ref,
    edges_ref,
    own_ref,
    senders_ref,
    receivers_ref,
    table_ref,
    second_ref,
    gain_ref,
    edges_out_ref,
    partial_ref,
    message_ref,
    total_ref,
):
    step = pl.program_id(0)
    rows = edges_ref.shape[0]
    receiver_count = partial_ref.shape[0]

    @pl.when(step == 0)
    def _():
        total_ref[...] = jnp.zeros_like(total_ref)

    count = counts_ref[0, 0]
    gain = gain_ref[...]
    for part in range(rows // chunk):
        span = pl.ds(part * chunk, chunk)
        ids = columns_of([senders_ref[:, span], receivers_ref[:, span]])
        chosen = jnp.concatenate(
            [hot(ids[:, 0:1], sender_count), hot(ids[:, 1:2], receiver_count)], axis=1
        )
        values = edges_ref[span]
        half = own_ref[span].astype(F32) + dot(chosen, table_ref[...])
        message = scaled(dot(silu_half(half), second_ref[...]), gain).astype(BF16)
        message_ref[span] = message
        place = step * rows + part * chunk + lax.broadcasted_iota(jnp.int32, (chunk, 1), 0)
        kept = jnp.where(place < count, message.astype(F32), 0.0)
        edges_out_ref[span] = (values.astype(F32) + kept).astype(BF16)
    slots = step * rows + lax.broadcasted_iota(jnp.int32, (1, rows), 1)
    targets = jnp.where(slots < count, receivers_ref[...], -1)
    spread = (lax.broadcasted_iota(jnp.int32, (receiver_count, rows), 0) == targets).astype(F32).astype(BF16)
    total_ref[...] += dot(spread, message_ref[...])

    @pl.when(step == pl.num_programs(0) - 1)
    def _():
        partial_ref[...] = total_ref[...].astype(BF16)


def node_kernel(
    n_row,
    n_col,
    partial_ref,
    nodes_ref,
    w1_hbm,
    w2_hbm,
    gain_ref,
    rows_ref,
    nodes_out_ref,
    band_ref,
    w1_ref,
    w2_ref,
    near_ref,
    stage_ref,
    far_ref,
    picked_ref,
    load_sem,
    near_send,
    near_recv,
    far_send,
    far_recv,
    band_send,
    band_recv,
):
    row, col = lax.axis_index("row"), lax.axis_index("col")
    outer, inner = split_of(n_col)
    high, low = col // inner, lax.rem(col, inner)
    me = row * n_col + col
    n_dev = n_row * n_col
    block, width = nodes_ref.shape
    pieces = width // LANES
    per_peer = rows_ref.shape[0]
    tile = pieces * per_peer
    barrier = pltpu.get_barrier_semaphore()

    def device(index):
        return (index // n_col, lax.rem(index, n_col))

    def greet(k, carry):
        pl.semaphore_signal(barrier, inc=1, device_id=device(lax.rem(me + k, n_dev)), device_id_type=MESH)
        return carry

    lax.fori_loop(1, n_dev, greet, 0)
    load_first = pltpu.make_async_copy(w1_hbm, w1_ref, load_sem.at[0])
    load_second = pltpu.make_async_copy(w2_hbm, w2_ref, load_sem.at[1])
    load_first.start()
    load_second.start()
    pl.semaphore_wait(barrier, n_dev - 1)

    def sums(k, m):
        index = lax.rem(high + k, outer) * inner + lax.rem(low + m, inner)
        return partial_ref.at[pl.ds(pl.multiple_of(index * block, block), block)]

    def near_copy(k, m):
        return pltpu.make_async_remote_copy(
            sums(k, m),
            near_ref.at[k * inner + m],
            near_send.at[k * inner + m],
            near_recv.at[k * inner + m],
            device_id=(row, high * inner + lax.rem(low + m, inner)),
            device_id_type=MESH,
        )

    def far_copy(k):
        return pltpu.make_async_remote_copy(
            stage_ref.at[k],
            far_ref.at[k],
            far_send.at[k],
            far_recv.at[k],
            device_id=(row, lax.rem(high + k, outer) * inner + low),
            device_id_type=MESH,
        )

    order = list(range(1, outer)) + [0]
    for k in order:
        for m in range(1, inner):
            near_copy(k, m).start()
    count = n_dev * tile
    owner = lax.broadcasted_iota(jnp.int32, (count, n_dev), 0) // tile
    spread = (owner == lax.broadcasted_iota(jnp.int32, (count, n_dev), 1)).astype(F32).astype(BF16)
    wanted = lax.dot_general(
        spread,
        rows_ref[...].astype(F32).astype(BF16),
        (((1,), (1,)), ((), ())),
        preferred_element_type=F32,
    )
    which = lax.broadcasted_iota(jnp.int32, (count, per_peer), 0) % per_peer
    wanted = jnp.where(which == lax.broadcasted_iota(jnp.int32, (count, per_peer), 1), wanted, 0.0)
    wanted = jnp.sum(wanted, axis=1, keepdims=True)
    local = lax.broadcasted_iota(jnp.int32, (count, block), 1).astype(F32)
    select = (local == wanted).astype(F32).astype(BF16)
    piece_of = (lax.broadcasted_iota(jnp.int32, (count, LANES), 0) // per_peer) % pieces

    total = None
    for k in order:
        total = sums(k, 0)[...].astype(F32)
        for m in range(1, inner):
            near_copy(k, m).wait()
            total = total + near_ref[k * inner + m].astype(F32)
        if k > 0:
            stage_ref[k] = total.astype(BF16)
            far_copy(k).start()
    load_first.wait()
    load_second.wait()
    base = dot(nodes_ref[...], halved(w1_ref[0]))
    lower = halved(w1_ref[1])
    second = centred(w2_ref[...])
    for k in range(1, outer):
        far_copy(k).wait()
        total = total + far_ref[k].astype(F32)
    half = base + dot(total.astype(BF16), lower)
    fresh = scaled(dot(silu_half(half), second), gain_ref[...])
    fresh = (nodes_ref[...].astype(F32) + fresh).astype(BF16)
    nodes_out_ref[...] = fresh
    selected = jnp.zeros((count, LANES), F32)
    for c in range(pieces):
        selected = jnp.where(piece_of == c, dot(select, fresh[:, c * LANES : (c + 1) * LANES]), selected)
    picked_ref[...] = selected.astype(BF16)

    def part(ref, index):
        return ref.at[pl.ds(pl.multiple_of(index * tile, tile), tile)]

    def send(k, carry):
        other = lax.rem(me + k, n_dev)
        pltpu.make_async_remote_copy(
            part(picked_ref, other),
            part(band_ref, me),
            band_send.at[k],
            band_recv.at[k],
            device_id=device(other),
            device_id_type=MESH,
        ).start()
        return carry

    lax.fori_loop(1, n_dev, send, 0)
    part(band_ref, me)[...] = part(picked_ref, me)[...]

    def finish(k, carry):
        other = lax.rem(me + k, n_dev)
        source = lax.rem(me + n_dev - k, n_dev)
        pltpu.make_async_remote_copy(
            part(picked_ref, other),
            part(band_ref, source),
            band_send.at[k],
            band_recv.at[k],
            device_id=device(other),
            device_id_type=MESH,
        ).wait()
        return carry

    lax.fori_loop(1, n_dev, finish, 0)


def grid_kernel(
    per_peer,
    grid_ref,
    index_ref,
    band_ref,
    w1_ref,
    w2_ref,
    gain_ref,
    nodes_ref,
    out_ref,
    nodes_out_ref,
    first_ref,
    second_ref,
    table_ref,
):
    count = table_ref.shape[0]
    pieces = grid_ref.shape[1] // LANES
    tile = pieces * per_peer

    @pl.when(pl.program_id(0) == 0)
    def _():
        nodes_out_ref[...] = nodes_ref[...]
        first_ref[...] = halved(w1_ref[0])
        second_ref[...] = centred(w2_ref[...])
        shape = (count, count * pieces)
        sender = lax.broadcasted_iota(jnp.int32, shape, 0)
        start = sender // per_peer * tile + sender % per_peer
        place = lax.broadcasted_iota(jnp.int32, shape, 1)
        band = band_ref[...]
        table = jnp.zeros(table_ref.shape, F32)
        for c in range(pieces):
            order = (place == start + c * per_peer).astype(F32).astype(BF16)
            piece = dot(order, band).astype(BF16)
            table = table + dot(piece, halved(w1_ref[1, c * LANES : (c + 1) * LANES]))
        table_ref[...] = table.astype(BF16)

    values = grid_ref[...]
    gain = gain_ref[...]
    fan = index_ref.shape[0]
    ids = columns_of([index_ref[e : e + 1] for e in range(fan)])
    base = dot(values, first_ref[...])
    total = values.astype(F32)
    for e in range(fan):
        half = base + dot(hot(ids[:, e : e + 1], count), table_ref[...])
        total = total + scaled(dot(silu_half(half), second_ref[...]), gain)
    out_ref[...] = total.astype(BF16)


def whole(shape):
    return pl.BlockSpec(shape, lambda i: (0,) * len(shape))


def on_device(
    n_row,
    n_col,
    nodes,
    edges,
    senders,
    receivers,
    levels,
    counts,
    edge_w1,
    level_bias,
    edge_w2,
    edge_gain,
    node_w1,
    node_w2,
    node_gain,
    grid,
    send_rows,
    dec_index,
    dec_w1,
    dec_w2,
    dec_gain,
):
    block, width = nodes.shape
    capacity = edges.shape[2]
    n_dev = n_row * n_col
    sender_count, receiver_count = block * n_row, block * n_col
    known = sender_count + receiver_count

    rows = math.gcd(capacity, 1024)
    chunk = math.gcd(rows, 256)
    stages = capacity // rows
    flat = edges.reshape(capacity, width)
    outer, inner = split_of(n_col)
    copies = n_row + n_col

    table, second, own = pl.pallas_call(
        functools.partial(gather_kernel, n_row, n_col),
        out_shape=(
            jax.ShapeDtypeStruct((known, width), BF16),
            jax.ShapeDtypeStruct((width, width), BF16),
            jax.ShapeDtypeStruct((capacity, width), BF16),
        ),
        in_specs=[VMEM, ANY, VMEM, ANY, VMEM, ANY],
        out_specs=(VMEM, VMEM, ANY),
        scratch_shapes=[
            pltpu.VMEM((known, width), BF16),
            pltpu.VMEM(edge_w1.shape, BF16),
            pltpu.VMEM(edge_w2.shape, BF16),
            pltpu.VMEM((stages, rows, width), BF16),
            pltpu.VMEM((stages, rows, width), BF16),
            pltpu.SemaphoreType.DMA((copies,)),
            pltpu.SemaphoreType.DMA((copies,)),
            pltpu.SemaphoreType.DMA((2,)),
            pltpu.SemaphoreType.DMA((stages,)),
            pltpu.SemaphoreType.DMA((stages,)),
        ],
        compiler_params=pltpu.CompilerParams(
            collective_id=0, has_side_effects=True, vmem_limit_bytes=VMEM_LIMIT
        ),
        name="gather_nodes",
    )(nodes, flat, levels.reshape(1, capacity), edge_w1, level_bias, edge_w2)

    def id_spec():
        return pl.BlockSpec((1, rows), lambda i: (0, i))

    edge_new, partial = pl.pallas_call(
        functools.partial(edge_kernel, sender_count, chunk),
        grid=(capacity // rows,),
        out_shape=(
            jax.ShapeDtypeStruct((capacity, width), BF16),
            jax.ShapeDtypeStruct((receiver_count, width), BF16),
        ),
        in_specs=[
            pl.BlockSpec(memory_space=pltpu.SMEM),
            pl.BlockSpec((rows, width), lambda i: (i, 0)),
            pl.BlockSpec((rows, width), lambda i: (i, 0)),
            id_spec(),
            id_spec(),
            whole((known, width)),
            whole((width, width)),
            whole((1, width)),
        ],
        out_specs=(pl.BlockSpec((rows, width), lambda i: (i, 0)), whole((receiver_count, width))),
        scratch_shapes=[
            pltpu.VMEM((rows, width), BF16),
            pltpu.VMEM((receiver_count, width), F32),
        ],
        compiler_params=pltpu.CompilerParams(vmem_limit_bytes=VMEM_LIMIT),
        name="edge_update",
    )(
        counts,
        flat,
        own,
        senders.reshape(1, capacity),
        receivers.reshape(1, capacity),
        table,
        second,
        edge_gain.reshape(1, width),
    )

    peers, per_peer = send_rows.shape[1:]
    tile = per_peer * (width // LANES)
    fresh_nodes, band = pl.pallas_call(
        functools.partial(node_kernel, n_row, n_col),
        out_shape=(
            jax.ShapeDtypeStruct((block, width), BF16),
            jax.ShapeDtypeStruct((peers * tile, LANES), BF16),
        ),
        in_specs=[VMEM, VMEM, ANY, ANY, VMEM, VMEM],
        out_specs=(VMEM, VMEM),
        scratch_shapes=[
            pltpu.VMEM(node_w1.shape, BF16),
            pltpu.VMEM(node_w2.shape, BF16),
            pltpu.VMEM((n_col, block, width), BF16),
            pltpu.VMEM((outer, block, width), BF16),
            pltpu.VMEM((outer, block, width), BF16),
            pltpu.VMEM((peers * tile, LANES), BF16),
            pltpu.SemaphoreType.DMA((2,)),
            pltpu.SemaphoreType.DMA((n_col,)),
            pltpu.SemaphoreType.DMA((n_col,)),
            pltpu.SemaphoreType.DMA((outer,)),
            pltpu.SemaphoreType.DMA((outer,)),
            pltpu.SemaphoreType.DMA((n_dev,)),
            pltpu.SemaphoreType.DMA((n_dev,)),
        ],
        compiler_params=pltpu.CompilerParams(
            collective_id=1, has_side_effects=True, vmem_limit_bytes=VMEM_LIMIT
        ),
        name="node_update",
    )(partial, nodes, node_w1, node_w2, node_gain.reshape(1, width), send_rows[0].T)

    cells, fan = dec_index.shape
    cell_rows = math.gcd(cells, 512)
    grid_out, nodes_out = pl.pallas_call(
        functools.partial(grid_kernel, per_peer),
        grid=(cells // cell_rows,),
        out_shape=(
            jax.ShapeDtypeStruct((cells, width), BF16),
            jax.ShapeDtypeStruct((block, width), BF16),
        ),
        in_specs=[
            pl.BlockSpec((cell_rows, width), lambda i: (i, 0)),
            pl.BlockSpec((fan, cell_rows), lambda i: (0, i)),
            whole((peers * tile, LANES)),
            whole(dec_w1.shape),
            whole(dec_w2.shape),
            whole((1, width)),
            whole((block, width)),
        ],
        out_specs=(pl.BlockSpec((cell_rows, width), lambda i: (i, 0)), whole((block, width))),
        scratch_shapes=[
            pltpu.VMEM((width, width), BF16),
            pltpu.VMEM((width, width), BF16),
            pltpu.VMEM((peers * per_peer, width), BF16),
        ],
        compiler_params=pltpu.CompilerParams(vmem_limit_bytes=VMEM_LIMIT),
        name="grid_update",
    )(grid, dec_index.T, band, dec_w1, dec_w2, dec_gain.reshape(1, width), fresh_nodes)
    return (nodes_out, edge_new.reshape(edges.shape), grid_out)


def solution(mesh):
    return jax.shard_map(
        functools.partial(on_device, mesh.shape["row"], mesh.shape["col"]),
        mesh=mesh,
        in_specs=(
            P(("row", "col"), None),
            P("row", "col", None, None),
            P("row", "col", None),
            P("row", "col", None),
            P("row", "col", None),
            P("row", "col"),
            P(),
            P(),
            P(),
            P(),
            P(),
            P(),
            P(),
            P(("row", "col"), None),
            P(("row", "col"), None, None),
            P(("row", "col"), None),
            P(),
            P(),
            P(),
        ),
        out_specs=(P(("row", "col"), None), P("row", "col", None, None), P(("row", "col"), None)),
        check_vma=False,
    )
```
